512 devices in a mesh: cube: 128 (over z, y, core), row: 4 (over x).
Axes of the slice: x: 4, y: 4, z: 16, core: 2. Of those that a mesh axis runs over, the one named last changes fastest.
Arguments:
- fronts: bfloat16 [128, 256, 16384], P('cube', None, 'row'), may hold values from -0.046875 to 0.046875
- omega: bfloat16 [128, 16384, 256], P('cube', 'row'), may hold values from -6 to 6
- leaf_sizes: int32 [128], P('cube'), may hold values from 64 to 256, as said below
- leaf_map: int32 [128, 256], P('cube'), may hold values from 0 to 511, as said below
- own_one: bfloat16 [128, 256, 256], P('cube', 'row'), may hold values from -6 to 6
- parent_count: int32 [128], P('cube'), may hold values from 64 to 256, as said below
- parent_map: int32 [128, 256], P('cube'), may hold values from 0 to 1023, as said below
- own_two: bfloat16 [128, 256, 256], P('cube', 'row'), may hold values from -6 to 6
Outputs:
- level_one: bfloat16 [128, 256, 256], P('cube', 'row')
- level_two: bfloat16 [128, 256, 256], P('cube', 'row')
The draws below stay inside these ranges and needn't reach their ends.
Inputs may be any that keep to these rules, and one draw needn't show every extreme that they name: `leaf_sizes`: some leaf has all 256 rows live. `leaf_map`: the rows of one leaf map to distinct parent rows. `parent_count`: some half has all 256 rows live. `parent_map`: the 512 rows of one level-one parent map to distinct level-two rows.
All inputs are finite; a program needn't handle non-finite values.
Results may differ from the reference program's by a relative error of at most 0.0039.
Values may be sent and summed in bfloat16 or wider, within the bound.
No kernel may reach another device: no remote copies, remote signals or barrier semaphores. Data moves between devices by JAX's collectives and lax.ppermute only.
A program may use at most 64 MiB of HBM per device.

```python
import jax
import jax.numpy as jnp
from jax import lax

LF = 16384
S = 256
RB = 256
PR1 = 512
PR2 = 1024
N_CUBE = 128


def draw_leaf_sizes(key, part):
    key = jax.random.fold_in(key, 11)
    first, second = jax.random.split(key)
    sizes = jax.random.randint(first, (N_CUBE,), RB // 4, RB + 1)
    place = jax.random.randint(second, (), 0, N_CUBE)
    return sizes.at[place].set(RB).astype(jnp.int32)


def draw_leaf_map(key, part):
    key = jax.random.fold_in(key, 12)
    keys = jax.random.split(key, N_CUBE)
    return jax.vmap(lambda k: jax.random.permutation(k, PR1)[:RB])(keys).astype(jnp.int32)


def draw_parent_count(key, part):
    key = jax.random.fold_in(key, 13)
    first, second = jax.random.split(key)
    sizes = jax.random.randint(first, (N_CUBE,), RB // 4, RB + 1)
    place = jax.random.randint(second, (), 0, N_CUBE)
    return sizes.at[place].set(RB).astype(jnp.int32)


def draw_parent_map(key, part):
    key = jax.random.fold_in(key, 14)
    keys = jax.random.split(key, N_CUBE // 2)
    picked = jax.vmap(lambda k: jax.random.permutation(k, PR2)[:PR1])(keys)
    return picked.reshape(N_CUBE, RB).astype(jnp.int32)


def shard_levels(stream_key, dims, cuts, smallest, largest):
    factor_of = 1.0
    for dim, parts in cuts:
        steps = jax.random.uniform(jax.random.fold_in(jax.random.fold_in(stream_key, 6), dim), (parts,), jnp.float32, smallest / len(cuts), largest / len(cuts))
        factor_of = factor_of * jnp.repeat(jnp.exp(steps), dims[dim] // parts).reshape((-1,) + (1,) * (len(dims) - 1 - dim))
    return factor_of


def normal_values(own_key, dims, spread, limit, cuts=(), kind=jnp.bfloat16):
    loudness = shard_levels(own_key, dims, cuts, -0.22, 0.18) if cuts else 1.0
    array = jax.random.normal(own_key, dims, jnp.float32) * spread * loudness
    return jnp.minimum(jnp.maximum(array, -limit), limit).astype(kind)


def setup_inputs(seed: int = 0) -> dict:
    key_of = jax.random.split(jax.random.key(seed), 9)
    fronts = normal_values(key_of[0], (N_CUBE, RB, LF), LF ** -0.5, 0.046875, ((0, 128), (2, 4)))
    omega = normal_values(key_of[1], (N_CUBE, LF, S), 1.0, 6.0, ((0, 128), (1, 4)))
    leaf_sizes = draw_leaf_sizes(jax.random.fold_in(key_of[8], 71), 0)
    leaf_map = draw_leaf_map(jax.random.fold_in(key_of[8], 71), 0)
    own_one = normal_values(key_of[4], (N_CUBE, RB, S), 1.0, 6.0, ((0, 128), (1, 4)))
    parent_count = draw_parent_count(jax.random.fold_in(key_of[8], 71), 0)
    parent_map = draw_parent_map(jax.random.fold_in(key_of[8], 71), 0)
    own_two = normal_values(key_of[7], (N_CUBE, RB, S), 1.0, 6.0, ((0, 128), (1, 4)))
    return {"fronts": fronts, "omega": omega, "leaf_sizes": leaf_sizes, "leaf_map": leaf_map, "own_one": own_one, "parent_count": parent_count, "parent_map": parent_map, "own_two": own_two}


def leaf_product(pair):
    block, sample = pair
    return jnp.dot(block, sample, preferred_element_type=jnp.float32).astype(jnp.bfloat16)


def reference(fronts, omega, leaf_sizes, leaf_map, own_one, parent_count, parent_map, own_two):
    samples = lax.map(leaf_product, (fronts, omega))
    count = fronts.shape[0]
    rows = fronts.shape[1]
    live = jnp.arange(rows, dtype=jnp.int32)[None, :] < leaf_sizes[:, None]
    contrib = jnp.where(live[:, :, None], samples.astype(jnp.float32), jnp.float32(0.0))
    parents = own_one.astype(jnp.float32).reshape(count // 2, 2 * rows, S)
    owner = jnp.broadcast_to((jnp.arange(count, dtype=jnp.int32) // 2)[:, None], (count, rows))
    parents = parents.at[owner, leaf_map].add(contrib)
    level_one = parents.astype(jnp.bfloat16).reshape(count, rows, S)
    live_two = jnp.arange(rows, dtype=jnp.int32)[None, :] < parent_count[:, None]
    contrib_two = jnp.where(live_two[:, :, None], level_one.astype(jnp.float32), jnp.float32(0.0))
    grand = own_two.astype(jnp.float32).reshape(count // 4, 4 * rows, S)
    owner_two = jnp.broadcast_to((jnp.arange(count, dtype=jnp.int32) // 4)[:, None], (count, rows))
    grand = grand.at[owner_two, parent_map].add(contrib_two)
    level_two = grand.astype(jnp.bfloat16).reshape(count, rows, S)
    return level_one, level_two
```

```python
import jax
import jax.numpy as jnp
from jax import lax
from jax.experimental import pallas as pl
from jax.experimental.pallas import tpu as pltpu
from jax.sharding import Mesh, PartitionSpec as P

CHUNKS = 4
DIGIT = 32
CODE_ROWS = 16
LIMIT = 32 * 2**20


def whole(memory):
    return pl.BlockSpec(memory_space=memory)


def product_kernel(fronts, omega, own, leaf_map, parent_map, leaf_size, count, out, a, b, sems):
    depth = a.shape[1] // CHUNKS
    rows = a.shape[0]
    copies = []
    for k in range(CHUNKS):
        part = pl.ds(k * depth, depth)
        copies.append(
            (
                pltpu.make_async_copy(fronts.at[0, :, part], a.at[:, part], sems.at[0, k]),
                pltpu.make_async_copy(omega.at[0, part, :], b.at[part, :], sems.at[1, k]),
            )
        )
        for copy in copies[-1]:
            copy.start()
    place = lax.broadcasted_iota(jnp.int32, (1, rows), 1)
    leaf = jnp.where(place < leaf_size[0], leaf_map[...], -1)
    parent = jnp.where(place < count[0], parent_map[...], -1)
    line = lax.broadcasted_iota(jnp.int32, (CODE_ROWS, rows), 0)
    code = jnp.where(line < 2, leaf, parent)
    code = jnp.where(line % 2 == 0, code >> 5, code & (DIGIT - 1))
    mine = own.shape[1]
    out[rows : rows + mine, :] = own[0]
    out[rows + mine :, :] = code.astype(jnp.float32).astype(jnp.bfloat16)
    total = None
    for k in range(CHUNKS):
        part = pl.ds(k * depth, depth)
        for copy in copies[k]:
            copy.wait()
        term = jnp.dot(a[:, part], b[part, :], preferred_element_type=jnp.float32)
        total = term if total is None else total + term
    out[:rows, :] = total.astype(jnp.bfloat16)


def decode(code):
    digits = code.astype(jnp.float32)
    leaf = digits[0:1] * DIGIT + digits[1:2]
    parent = digits[2:3] * DIGIT + digits[3:4]
    return leaf.astype(jnp.int32), parent.astype(jnp.int32)


def place_kernel(mine, other, out, parents):
    rows = out.shape[2]
    block = out.shape[1] // 2
    n_row = rows // block
    core, row = lax.axis_index("core"), lax.axis_index("row")
    leaf_a, parent_a = decode(mine[rows + block :, :])
    leaf_b, parent_b = decode(other[rows + block :, :])
    line = lax.broadcasted_iota(jnp.int32, (2 * rows, rows), 0)
    parent_row = jnp.bitwise_xor(line, core * rows)
    pick_a = (parent_row == leaf_a).astype(jnp.bfloat16)
    pick_b = (parent_row == leaf_b).astype(jnp.bfloat16)
    summed = jnp.dot(pick_a, mine[:rows, :], preferred_element_type=jnp.float32)
    summed += jnp.dot(pick_b, other[:rows, :], preferred_element_type=jnp.float32)
    level_one = summed[:rows].astype(jnp.bfloat16)
    for y in range(2):
        for x in range(n_row):
            out[y * n_row + x, block:, :] = level_one[x * block : (x + 1) * block]
    parents[...] = summed
    first = pl.multiple_of(row * block, block)
    parents[pl.ds(first, block), :] += mine[rows : rows + block, :].astype(jnp.float32)
    parents[pl.ds(rows + first, block), :] += other[rows : rows + block, :].astype(jnp.float32)
    quarter = jnp.where(line < rows, line, line + rows) + core * rows
    pick_a = (quarter == parent_a).astype(jnp.bfloat16)
    pick_b = (quarter == parent_b).astype(jnp.bfloat16)
    upper = jnp.dot(pick_a, parents[:rows].astype(jnp.bfloat16), preferred_element_type=jnp.float32)
    upper += jnp.dot(pick_b, parents[rows:].astype(jnp.bfloat16), preferred_element_type=jnp.float32)
    upper = upper.astype(jnp.bfloat16)
    for k in range(2 * n_row):
        out[k, :block, :] = upper[k * block : (k + 1) * block]


def sum_kernel(pieces, own_one, own_two, one, two):
    n_row = pieces.shape[0] // 2
    block = own_one.shape[1]
    first = lax.axis_index("y") * n_row
    total = own_one[0].astype(jnp.float32)
    for x in range(n_row):
        total += pieces[first + x, block:, :].astype(jnp.float32)
    one[0] = total.astype(jnp.bfloat16)
    total = own_two[0].astype(jnp.float32)
    for k in range(2 * n_row):
        total += pieces[k, :block, :].astype(jnp.float32)
    two[0] = total.astype(jnp.bfloat16)


def body(fronts, omega, leaf_sizes, leaf_map, own_one, parent_count, parent_map, own_two):
    _, rows, depth = fronts.shape
    cols = omega.shape[2]
    block = own_one.shape[1]
    params = pltpu.CompilerParams(vmem_limit_bytes=LIMIT)
    vmem, smem = whole(pltpu.VMEM), whole(pltpu.SMEM)
    hbm = lambda array: pltpu.with_memory_space_constraint(array, pltpu.HBM)
    near = lambda array: pltpu.with_memory_space_constraint(array, pltpu.VMEM)
    message = pl.pallas_call(
        product_kernel,
        out_shape=pltpu.VMEM((rows + block + CODE_ROWS, cols), jnp.bfloat16),
        in_specs=[whole(pl.ANY), whole(pl.ANY), vmem, vmem, vmem, smem, smem],
        out_specs=vmem,
        scratch_shapes=[
            pltpu.VMEM((rows, depth), jnp.bfloat16),
            pltpu.VMEM((depth, cols), jnp.bfloat16),
            pltpu.SemaphoreType.DMA((2, CHUNKS)),
        ],
        compiler_params=params,
        name="product",
    )(hbm(fronts), hbm(omega), own_one, leaf_map, parent_map, leaf_sizes, parent_count)
    sibling = lax.ppermute(message, "core", [(0, 1), (1, 0)])
    n_row = rows // block
    pieces = pl.pallas_call(
        place_kernel,
        out_shape=pltpu.VMEM((2 * n_row, 2 * block, cols), jnp.bfloat16),
        in_specs=[vmem, vmem],
        out_specs=vmem,
        scratch_shapes=[pltpu.VMEM((2 * rows, cols), jnp.float32)],
        compiler_params=params,
        name="place",
    )(near(message), near(sibling))
    pieces = lax.all_to_all(pieces, ("y", "row"), 0, 0)
    shape = jax.ShapeDtypeStruct(own_one.shape, jnp.bfloat16)
    return pl.pallas_call(
        sum_kernel,
        out_shape=(shape, shape),
        in_specs=[vmem, vmem, vmem],
        out_specs=(vmem, vmem),
        compiler_params=params,
        name="total",
    )(near(pieces), own_one, own_two)


def solution(mesh):
    n_cube, n_row = mesh.devices.shape
    grouped = Mesh(mesh.devices.reshape(n_cube // 4, 2, 2, n_row), ("group", "y", "core", "row"))
    cube = ("group", "y", "core")
    in_specs = (
        P(cube, None, "row"),
        P(cube, "row", None),
        P(cube),
        P(cube, None),
        P(cube, "row", None),
        P(cube),
        P(cube, None),
        P(cube, "row", None),
    )
    out_specs = (P(cube, "row", None), P(cube, "row", None))
    return jax.shard_map(body, mesh=grouped, in_specs=in_specs, out_specs=out_specs, check_vma=False)
```

```python
import jax
import jax.numpy as jnp
from jax import lax
from jax.experimental import pallas as pl
from jax.experimental.pallas import tpu as pltpu
from jax.sharding import Mesh, PartitionSpec as P

CHUNKS = 4
DIGIT = 32
CODE_ROWS = 16
LIMIT = 32 * 2**20
COST = pl.CostEstimate(flops=8 * 10**9, bytes_accessed=2**24, transcendentals=0)


def whole(memory):
    return pl.BlockSpec(memory_space=memory)


def first_kernel(out):
    out[...] = jnp.zeros_like(out)


def product_kernel(blank, fronts, omega, own_one, own_two, leaf_map, parent_map, leaf_size, count, out, two):
    rows = fronts.shape[1]
    mine = own_one.shape[1]
    place = lax.broadcasted_iota(jnp.int32, (1, rows), 1)
    leaf = jnp.where(place < leaf_size[0], leaf_map[...], -1)
    parent = jnp.where(place < count[0], parent_map[...], -1)
    line = lax.broadcasted_iota(jnp.int32, (CODE_ROWS, rows), 0)
    code = jnp.where(line < 2, leaf, parent)
    code = jnp.where(line % 2 == 0, code >> 5, code & (DIGIT - 1))
    out[rows + mine :, :] = (code.astype(jnp.float32) + blank[...]).astype(jnp.bfloat16)
    out[rows : rows + mine, :] = own_one[0]
    two[...] = own_two[0]
    out[:rows, :] = jnp.dot(fronts[0], omega[0], preferred_element_type=jnp.float32).astype(jnp.bfloat16)


def decode(code):
    digits = code.astype(jnp.float32)
    leaf = digits[0:1] * DIGIT + digits[1:2]
    parent = digits[2:3] * DIGIT + digits[3:4]
    return leaf.astype(jnp.int32), parent.astype(jnp.int32)


def picks(blocks, index):
    rows = index.shape[1]
    line = lax.broadcasted_iota(jnp.int32, (rows, rows), 0)
    return jnp.concatenate([(line + block * rows == index).astype(jnp.bfloat16) for block in blocks], axis=0)


def own_place_kernel(mine, parents, upper):
    rows = parents.shape[0] // 2
    core = lax.axis_index("core")
    leaf, parent = decode(mine[mine.shape[0] - CODE_ROWS :, :])
    pick = picks((core, 1 - core), leaf)
    parents[...] = jnp.dot(pick, mine[:rows, :], preferred_element_type=jnp.float32).astype(jnp.bfloat16)
    upper[...] = picks((core, core + 2), parent)


def place_kernel(mine, other, placed, picked, out):
    rows = out.shape[2]
    block = out.shape[1] // 2
    n_row = rows // block
    core, row = lax.axis_index("core"), lax.axis_index("row")
    leaf, parent = decode(other[rows + block :, :])
    pick = picks((core, 1 - core), leaf)
    parents = jnp.dot(pick, other[:rows, :], preferred_element_type=jnp.float32) + placed[...].astype(jnp.float32)
    level_one = parents[:rows].astype(jnp.bfloat16)
    for x in range(n_row):
        out[x, block:, :] = level_one[x * block : (x + 1) * block]
        out[n_row + x, block:, :] = level_one[x * block : (x + 1) * block]
    line = lax.broadcasted_iota(jnp.int32, (rows, 1), 0) // block == row
    own = jnp.concatenate([mine[rows : rows + block, :]] * n_row, axis=0).astype(jnp.float32)
    lower = (parents[:rows] + jnp.where(line, own, 0.0)).astype(jnp.bfloat16)
    upper = jnp.dot(picked[...], lower, preferred_element_type=jnp.float32)
    own = jnp.concatenate([other[rows : rows + block, :]] * n_row, axis=0).astype(jnp.float32)
    lower = (parents[rows:] + jnp.where(line, own, 0.0)).astype(jnp.bfloat16)
    upper += jnp.dot(picks((core, core + 2), parent), lower, preferred_element_type=jnp.float32)
    upper = upper.astype(jnp.bfloat16)
    for k in range(2 * n_row):
        out[k, :block, :] = upper[k * block : (k + 1) * block]


def sum_kernel(pieces, message, own_two, one, two):
    n_row, rows = pieces.shape[0] // 2, pieces.shape[2]
    block = own_two.shape[0]
    first = lax.axis_index("y") * n_row
    total = message[rows : rows + block, :].astype(jnp.float32)
    for x in range(n_row):
        total += pieces[first + x, block:, :].astype(jnp.float32)
    one[0] = total.astype(jnp.bfloat16)
    total = own_two[...].astype(jnp.float32)
    for k in range(2 * n_row):
        total += pieces[k, :block, :].astype(jnp.float32)
    two[0] = total.astype(jnp.bfloat16)


def body(fronts, omega, leaf_sizes, leaf_map, own_one, parent_count, parent_map, own_two):
    _, rows, depth = fronts.shape
    cols = omega.shape[2]
    block = own_one.shape[1]
    params = pltpu.CompilerParams(vmem_limit_bytes=LIMIT)
    vmem, smem = whole(pltpu.VMEM), whole(pltpu.SMEM)
    hbm = lambda array: pltpu.with_memory_space_constraint(array, pltpu.HBM)
    near = lambda array: pltpu.with_memory_space_constraint(array, pltpu.VMEM)
    blank = pl.pallas_call(
        first_kernel,
        out_shape=pltpu.VMEM((CODE_ROWS, cols), jnp.float32),
        in_specs=[],
        out_specs=vmem,
        compiler_params=params,
        cost_estimate=COST,
        name="first",
    )()
    message, late = pl.pallas_call(
        product_kernel,
        out_shape=(pltpu.VMEM((rows + block + CODE_ROWS, cols), jnp.bfloat16), pltpu.VMEM((block, cols), jnp.bfloat16)),
        in_specs=[vmem] * 7 + [smem, smem],
        out_specs=(vmem, vmem),
        compiler_params=params,
        name="product",
    )(near(blank), fronts, omega, own_one, own_two, leaf_map, parent_map, leaf_sizes, parent_count)
    sibling = lax.ppermute(message, "core", [(0, 1), (1, 0)])
    n_row = rows // block
    placed, picked = pl.pallas_call(
        own_place_kernel,
        out_shape=(pltpu.VMEM((2 * rows, cols), jnp.bfloat16), pltpu.VMEM((2 * rows, rows), jnp.bfloat16)),
        in_specs=[vmem],
        out_specs=(vmem, vmem),
        compiler_params=params,
        cost_estimate=pl.CostEstimate(flops=4 * rows * rows * cols, bytes_accessed=2**20, transcendentals=0),
        name="own_place",
    )(near(message))
    pieces = pl.pallas_call(
        place_kernel,
        out_shape=pltpu.VMEM((2 * n_row, 2 * block, cols), jnp.bfloat16),
        in_specs=[vmem] * 4,
        out_specs=vmem,
        compiler_params=params,
        name="place",
    )(near(message), near(sibling), near(placed), near(picked))
    pieces = lax.all_to_all(pieces, ("y", "row"), 0, 0)
    shape = jax.ShapeDtypeStruct(own_one.shape, jnp.bfloat16)
    return pl.pallas_call(
        sum_kernel,
        out_shape=(shape, shape),
        in_specs=[vmem, vmem, vmem],
        out_specs=(vmem, vmem),
        compiler_params=params,
        name="total",
    )(near(pieces), near(message), near(late))


def solution(mesh):
    n_cube, n_row = mesh.devices.shape
    grouped = Mesh(mesh.devices.reshape(n_cube // 4, 2, 2, n_row), ("group", "y", "core", "row"))
    cube = ("group", "y", "core")
    in_specs = (
        P(cube, None, "row"),
        P(cube, "row", None),
        P(cube),
        P(cube, None),
        P(cube, "row", None),
        P(cube),
        P(cube, None),
        P(cube, "row", None),
    )
    out_specs = (P(cube, "row", None), P(cube, "row", None))
    return jax.shard_map(body, mesh=grouped, in_specs=in_specs, out_specs=out_specs, check_vma=False)
```

```python
import jax
import jax.numpy as jnp
from jax import lax
from jax.experimental import pallas as pl
from jax.experimental.pallas import tpu as pltpu
from jax.sharding import Mesh, PartitionSpec as P

DIGIT = 32
CODE_ROWS = 16
LIMIT = 32 * 2**20


def whole(memory):
    return pl.BlockSpec(memory_space=memory)


def picks(blocks, index):
    rows = index.shape[1]
    line = lax.broadcasted_iota(jnp.int32, (rows, rows), 0)
    return jnp.concatenate([(line + block * rows == index).astype(jnp.bfloat16) for block in blocks], axis=0)


def first_kernel(out):
    out[...] = jnp.zeros_like(out)


def product_kernel(blank, fronts, omega, own_one, own_two, leaf_map, parent_map, leaf_size, count, out, two, lower, upper):
    rows = fronts.shape[1]
    mine = own_one.shape[1]
    core = lax.axis_index("core")
    place = lax.broadcasted_iota(jnp.int32, (1, rows), 1)
    leaf = jnp.where(place < leaf_size[0], leaf_map[...], -1)
    parent = jnp.where(place < count[0], parent_map[...], -1)
    line = lax.broadcasted_iota(jnp.int32, (CODE_ROWS, rows), 0)
    code = jnp.where(line < 2, leaf, parent)
    code = jnp.where(line % 2 == 0, code >> 5, code & (DIGIT - 1))
    out[rows + mine :, :] = (code.astype(jnp.float32) + blank[...]).astype(jnp.bfloat16)
    out[rows : rows + mine, :] = own_one[0]
    two[...] = own_two[0]
    lower[...] = picks((core, 1 - core), leaf)
    upper[...] = picks((core, core + 2), parent)
    out[:rows, :] = jnp.dot(fronts[0], omega[0], preferred_element_type=jnp.float32).astype(jnp.bfloat16)


def decode(code):
    digits = code.astype(jnp.float32)
    leaf = digits[0:1] * DIGIT + digits[1:2]
    parent = digits[2:3] * DIGIT + digits[3:4]
    return leaf.astype(jnp.int32), parent.astype(jnp.int32)


def place_kernel(mine, both, lower, upper, out):
    rows = out.shape[2]
    block = out.shape[1] // 2
    n_row = rows // block
    core, row = lax.axis_index("core"), lax.axis_index("row")
    other = both.at[1 - core]
    leaf, parent = decode(other[rows + block :, :])
    parents = jnp.dot(lower[...], mine[:rows, :], preferred_element_type=jnp.float32)
    parents += jnp.dot(picks((core, 1 - core), leaf), other[:rows, :], preferred_element_type=jnp.float32)
    level_one = parents[:rows].astype(jnp.bfloat16)
    for x in range(n_row):
        for y in range(2):
            out[2 * x + y, block:, :] = level_one[x * block : (x + 1) * block]
    line = lax.broadcasted_iota(jnp.int32, (rows, 1), 0) // block == row
    own = jnp.concatenate([mine[rows : rows + block, :]] * n_row, axis=0).astype(jnp.float32)
    half = (parents[:rows] + jnp.where(line, own, 0.0)).astype(jnp.bfloat16)
    placed = jnp.dot(upper[...], half, preferred_element_type=jnp.float32)
    own = jnp.concatenate([other[rows : rows + block, :]] * n_row, axis=0).astype(jnp.float32)
    half = (parents[rows:] + jnp.where(line, own, 0.0)).astype(jnp.bfloat16)
    placed += jnp.dot(picks((core, core + 2), parent), half, preferred_element_type=jnp.float32)
    placed = placed.astype(jnp.bfloat16)
    for x in range(n_row):
        for y in range(2):
            out[2 * x + y, :block, :] = placed[y * rows + x * block : y * rows + (x + 1) * block]


def sum_kernel(pieces, message, own_two, one, two):
    n_row, rows = pieces.shape[0] // 2, pieces.shape[2]
    block = own_two.shape[0]
    y = lax.axis_index("y")
    total = message[rows : rows + block, :].astype(jnp.float32)
    for x in range(n_row):
        total += pieces[2 * x + y, block:, :].astype(jnp.float32)
    one[0] = total.astype(jnp.bfloat16)
    total = own_two[...].astype(jnp.float32)
    for k in range(2 * n_row):
        total += pieces[k, :block, :].astype(jnp.float32)
    two[0] = total.astype(jnp.bfloat16)


def body(fronts, omega, leaf_sizes, leaf_map, own_one, parent_count, parent_map, own_two):
    _, rows, depth = fronts.shape
    cols = omega.shape[2]
    block = own_one.shape[1]
    n_row = rows // block
    params = pltpu.CompilerParams(vmem_limit_bytes=LIMIT)
    vmem, smem = whole(pltpu.VMEM), whole(pltpu.SMEM)
    near = lambda array: pltpu.with_memory_space_constraint(array, pltpu.VMEM)
    blank = pl.pallas_call(
        first_kernel,
        out_shape=pltpu.VMEM((CODE_ROWS, cols), jnp.float32),
        in_specs=[],
        out_specs=vmem,
        compiler_params=params,
        cost_estimate=pl.CostEstimate(flops=8 * 10**9, bytes_accessed=2**24, transcendentals=0),
        name="first",
    )()
    pick = pltpu.VMEM((2 * rows, rows), jnp.bfloat16)
    message, late, lower, upper = pl.pallas_call(
        product_kernel,
        out_shape=(
            pltpu.VMEM((rows + block + CODE_ROWS, cols), jnp.bfloat16),
            pltpu.VMEM((block, cols), jnp.bfloat16),
            pick,
            pick,
        ),
        in_specs=[vmem] * 7 + [smem, smem],
        out_specs=(vmem,) * 4,
        compiler_params=params,
        name="product",
    )(near(blank), fronts, omega, own_one, own_two, leaf_map, parent_map, leaf_sizes, parent_count)
    both = lax.all_gather(message, "core")
    pieces = pl.pallas_call(
        place_kernel,
        out_shape=pltpu.VMEM((2 * n_row, 2 * block, cols), jnp.bfloat16),
        in_specs=[vmem] * 4,
        out_specs=vmem,
        compiler_params=params,
        name="place",
    )(near(message), near(both), near(lower), near(upper))
    pieces = lax.all_to_all(pieces, ("row", "y"), 0, 0)
    shape = jax.ShapeDtypeStruct(own_one.shape, jnp.bfloat16)
    return pl.pallas_call(
        sum_kernel,
        out_shape=(shape, shape),
        in_specs=[vmem, vmem, vmem],
        out_specs=(vmem, vmem),
        compiler_params=params,
        name="total",
    )(near(pieces), near(message), near(late))


def solution(mesh):
    n_cube, n_row = mesh.devices.shape
    grouped = Mesh(mesh.devices.reshape(n_cube // 4, 2, 2, n_row), ("group", "y", "core", "row"))
    cube = ("group", "y", "core")
    in_specs = (
        P(cube, None, "row"),
        P(cube, "row", None),
        P(cube),
        P(cube, None),
        P(cube, "row", None),
        P(cube),
        P(cube, None),
        P(cube, "row", None),
    )
    out_specs = (P(cube, "row", None), P(cube, "row", None))
    return jax.shard_map(body, mesh=grouped, in_specs=in_specs, out_specs=out_specs, check_vma=False)
```

```python
import jax
import jax.numpy as jnp
from jax import lax
from jax.experimental import pallas as pl
from jax.experimental.pallas import tpu as pltpu
from jax.sharding import Mesh, PartitionSpec as P

DIGIT = 32
CODE_ROWS = 16
LIMIT = 32 * 2**20


def whole(memory):
    return pl.BlockSpec(memory_space=memory)


def picks(blocks, index):
    rows = index.shape[1]
    line = lax.broadcasted_iota(jnp.int32, (rows, rows), 0)
    return jnp.concatenate([(line + block * rows == index).astype(jnp.bfloat16) for block in blocks], axis=0)


def first_kernel(out):
    out[...] = jnp.zeros_like(out)


def index_kernel(blank, leaf_map, parent_map, leaf_size, count, code, lower, upper):
    rows = leaf_map.shape[1]
    core = lax.axis_index("core")
    place = lax.broadcasted_iota(jnp.int32, (1, rows), 1)
    leaf = jnp.where(place < leaf_size[0], leaf_map[...], -1)
    parent = jnp.where(place < count[0], parent_map[...], -1)
    line = lax.broadcasted_iota(jnp.int32, (CODE_ROWS, rows), 0)
    digits = jnp.where(line < 2, leaf, parent)
    digits = jnp.where(line % 2 == 0, digits >> 5, digits & (DIGIT - 1))
    code[...] = (digits.astype(jnp.float32) + blank[...]).astype(jnp.bfloat16)
    lower[...] = picks((core, 1 - core), leaf)
    upper[...] = picks((core, core + 2), parent)


def product_kernel(fronts, omega, own_one, own_two, code, out, two):
    rows = fronts.shape[1]
    mine = own_one.shape[1]
    out[rows : rows + mine, :] = own_one[0]
    out[rows + mine :, :] = code[...]
    two[...] = own_two[0]
    out[:rows, :] = jnp.dot(fronts[0], omega[0], preferred_element_type=jnp.float32).astype(jnp.bfloat16)


def decode(code):
    digits = code.astype(jnp.float32)
    leaf = digits[0:1] * DIGIT + digits[1:2]
    parent = digits[2:3] * DIGIT + digits[3:4]
    return leaf.astype(jnp.int32), parent.astype(jnp.int32)


def place_kernel(mine, both, lower, upper, out):
    rows = out.shape[2]
    block = out.shape[1] // 2
    n_row = rows // block
    core, row, here = lax.axis_index("core"), lax.axis_index("row"), lax.axis_index("y")
    other = both.at[1 - core]
    leaf, parent = decode(other[rows + block :, :])
    other_lower, other_upper = picks((core, 1 - core), leaf), picks((core, core + 2), parent)
    partial = jnp.concatenate([mine[:rows, :], other[:rows, :]], axis=0)
    line = lax.broadcasted_iota(jnp.int32, (rows, 1), 0) // block == row
    halves = []
    for k, source in enumerate((mine, other)):
        part = slice(k * rows, (k + 1) * rows)
        pick = jnp.concatenate([lower[part], other_lower[part]], axis=1)
        half = jnp.dot(pick, partial, preferred_element_type=jnp.float32)
        if k == 0:
            level_one = half.astype(jnp.bfloat16)
        own = jnp.concatenate([source[rows : rows + block, :]] * n_row, axis=0)
        halves.append(jnp.where(line, half + own.astype(jnp.float32), half).astype(jnp.bfloat16))
    parents = jnp.concatenate(halves, axis=0)
    for x in range(n_row):
        out[2 * x + here, block:, :] = level_one[x * block : (x + 1) * block]
        out[2 * x + 1 - here, block:, :] = jnp.zeros((block, rows), jnp.bfloat16)
    for y in range(2):
        part = slice(y * rows, (y + 1) * rows)
        pick = jnp.concatenate([upper[part], other_upper[part]], axis=1)
        placed = jnp.dot(pick, parents, preferred_element_type=jnp.float32).astype(jnp.bfloat16)
        for x in range(n_row):
            out[2 * x + y, :block, :] = placed[x * block : (x + 1) * block]


def sum_kernel(pieces, message, own_two, one, two):
    n_row, rows = pieces.shape[0] // 2, pieces.shape[2]
    block = own_two.shape[0]
    y = lax.axis_index("y")
    total = message[rows : rows + block, :].astype(jnp.float32)
    for x in range(n_row):
        total += pieces[2 * x + y, block:, :].astype(jnp.float32)
    one[0] = total.astype(jnp.bfloat16)
    total = own_two[...].astype(jnp.float32)
    for k in range(2 * n_row):
        total += pieces[k, :block, :].astype(jnp.float32)
    two[0] = total.astype(jnp.bfloat16)


def body(fronts, omega, leaf_sizes, leaf_map, own_one, parent_count, parent_map, own_two):
    _, rows, depth = fronts.shape
    cols = omega.shape[2]
    block = own_one.shape[1]
    n_row = rows // block
    params = pltpu.CompilerParams(vmem_limit_bytes=LIMIT)
    vmem, smem = whole(pltpu.VMEM), whole(pltpu.SMEM)
    near = lambda array: pltpu.with_memory_space_constraint(array, pltpu.VMEM)
    blank = pl.pallas_call(
        first_kernel,
        out_shape=pltpu.VMEM((CODE_ROWS, cols), jnp.float32),
        in_specs=[],
        out_specs=vmem,
        compiler_params=params,
        cost_estimate=pl.CostEstimate(flops=8 * 10**9, bytes_accessed=2**24, transcendentals=0),
        name="first",
    )()
    pick = pltpu.VMEM((2 * rows, rows), jnp.bfloat16)
    code, lower, upper = pl.pallas_call(
        index_kernel,
        out_shape=(pltpu.VMEM((CODE_ROWS, rows), jnp.bfloat16), pick, pick),
        in_specs=[vmem] * 3 + [smem, smem],
        out_specs=(vmem,) * 3,
        compiler_params=params,
        name="index",
    )(near(blank), leaf_map, parent_map, leaf_sizes, parent_count)
    message, late = pl.pallas_call(
        product_kernel,
        out_shape=(
            pltpu.VMEM((rows + block + CODE_ROWS, cols), jnp.bfloat16),
            pltpu.VMEM((block, cols), jnp.bfloat16),
        ),
        in_specs=[vmem] * 5,
        out_specs=(vmem,) * 2,
        compiler_params=params,
        name="product",
    )(fronts, omega, own_one, own_two, near(code))
    both = lax.all_gather(message, "core")
    pieces = pl.pallas_call(
        place_kernel,
        out_shape=pltpu.VMEM((2 * n_row, 2 * block, cols), jnp.bfloat16),
        in_specs=[vmem] * 4,
        out_specs=vmem,
        compiler_params=params,
        name="place",
    )(near(message), near(both), near(lower), near(upper))
    pieces = lax.all_to_all(pieces, ("row", "y"), 0, 0)
    shape = jax.ShapeDtypeStruct(own_one.shape, jnp.bfloat16)
    return pl.pallas_call(
        sum_kernel,
        out_shape=(shape, shape),
        in_specs=[vmem, vmem, vmem],
        out_specs=(vmem, vmem),
        compiler_params=params,
        name="total",
    )(near(pieces), near(message), near(late))


def solution(mesh):
    n_cube, n_row = mesh.devices.shape
    grouped = Mesh(mesh.devices.reshape(n_cube // 4, 2, 2, n_row), ("group", "y", "core", "row"))
    cube = ("group", "y", "core")
    in_specs = (
        P(cube, None, "row"),
        P(cube, "row", None),
        P(cube),
        P(cube, None),
        P(cube, "row", None),
        P(cube),
        P(cube, None),
        P(cube, "row", None),
    )
    out_specs = (P(cube, "row", None), P(cube, "row", None))
    return jax.shard_map(body, mesh=grouped, in_specs=in_specs, out_specs=out_specs, check_vma=False)
```

```python
import jax
import jax.numpy as jnp
from jax import lax
from jax.experimental import pallas as pl
from jax.experimental.pallas import tpu as pltpu
from jax.sharding import Mesh, PartitionSpec as P

DIGIT = 32
CODE_ROWS = 16
LIMIT = 32 * 2**20


def whole(memory):
    return pl.BlockSpec(memory_space=memory)


def picks(blocks, index):
    rows = index.shape[1]
    line = lax.broadcasted_iota(jnp.int32, (rows, rows), 0)
    return jnp.concatenate([(line + block * rows == index).astype(jnp.bfloat16) for block in blocks], axis=0)


def first_kernel(out):
    out[...] = jnp.zeros_like(out)


def index_kernel(blank, leaf_map, parent_map, leaf_size, count, code, lower, upper):
    rows = leaf_map.shape[1]
    core = lax.axis_index("core")
    place = lax.broadcasted_iota(jnp.int32, (1, rows), 1)
    leaf = jnp.where(place < leaf_size[0], leaf_map[...], -1)
    parent = jnp.where(place < count[0], parent_map[...], -1)
    line = lax.broadcasted_iota(jnp.int32, (CODE_ROWS, rows), 0)
    digits = jnp.where(line < 2, leaf, parent)
    digits = jnp.where(line % 2 == 0, digits >> 5, digits & (DIGIT - 1))
    code[...] = (digits.astype(jnp.float32) + blank[...]).astype(jnp.bfloat16)
    lower[...] = picks((core, 1 - core), leaf)
    here = lax.axis_index("y")
    upper[...] = picks((core + 2 * here, core + 2 - 2 * here), parent)


def product_kernel(fronts, omega, own_one, own_two, code, out, rest, two):
    rows = fronts.shape[1]
    mine = own_one.shape[1]
    out[rows : rows + mine, :] = own_one[0]
    out[rows + mine :, :] = code[...]
    two[...] = own_two[0]
    partial = jnp.dot(fronts[0], omega[0], preferred_element_type=jnp.float32)
    high = partial.astype(jnp.bfloat16)
    out[:rows, :] = high
    rest[...] = (partial - high.astype(jnp.float32)).astype(jnp.bfloat16)


def decode(code):
    digits = code.astype(jnp.float32)
    leaf = digits[0:1] * DIGIT + digits[1:2]
    parent = digits[2:3] * DIGIT + digits[3:4]
    return leaf.astype(jnp.int32), parent.astype(jnp.int32)


def place_kernel(mine, rest, both, lower, upper, out):
    rows = out.shape[2]
    block = out.shape[1] // 2
    n_row = rows // block
    core, row, here = lax.axis_index("core"), lax.axis_index("row"), lax.axis_index("y")
    other = both.at[1 - core]
    leaf, parent = decode(other[rows + block :, :])
    other_lower = picks((core, 1 - core), leaf)
    other_upper = picks((core + 2 * here, core + 2 - 2 * here), parent)
    partial = jnp.concatenate([mine[:rows, :], rest[...], other[:rows, :]], axis=0)
    line = lax.broadcasted_iota(jnp.int32, (rows, 1), 0) // block == row
    highs, lows = [], []
    for k, source in enumerate((mine, other)):
        part = slice(k * rows, (k + 1) * rows)
        pick = jnp.concatenate([lower[part], lower[part], other_lower[part]], axis=1)
        half = jnp.dot(pick, partial, preferred_element_type=jnp.float32)
        if k == 0:
            level_one = half.astype(jnp.bfloat16)
        own = jnp.concatenate([source[rows : rows + block, :]] * n_row, axis=0)
        half = jnp.where(line, half + own.astype(jnp.float32), half)
        highs.append(half.astype(jnp.bfloat16))
        lows.append((half - highs[k].astype(jnp.float32)).astype(jnp.bfloat16))
    for x in range(n_row):
        out[2 * x + here, block:, :] = level_one[x * block : (x + 1) * block]
    high, low = jnp.concatenate(highs, axis=0), jnp.concatenate(lows, axis=0)
    for k, y in enumerate((here, 1 - here)):
        part = slice(k * rows, (k + 1) * rows)
        pick = jnp.concatenate([upper[part], other_upper[part]], axis=1)
        placed = jnp.dot(pick, high, preferred_element_type=jnp.float32).astype(jnp.bfloat16)
        for x in range(n_row):
            out[2 * x + y, :block, :] = placed[x * block : (x + 1) * block]
        if k == 1:
            placed = jnp.dot(pick, low, preferred_element_type=jnp.float32).astype(jnp.bfloat16)
            for x in range(n_row):
                out[2 * x + y, block:, :] = placed[x * block : (x + 1) * block]


def sum_kernel(pieces, message, own_two, one, two):
    n_row, rows = pieces.shape[0] // 2, pieces.shape[2]
    block = own_two.shape[0]
    y = lax.axis_index("y")
    total = message[rows : rows + block, :].astype(jnp.float32)
    for x in range(n_row):
        total += pieces[2 * x + y, block:, :].astype(jnp.float32)
    one[0] = total.astype(jnp.bfloat16)
    total = own_two[...].astype(jnp.float32)
    for k in range(2 * n_row):
        total += pieces[k, :block, :].astype(jnp.float32)
    for x in range(n_row):
        total += pieces[2 * x + 1 - y, block:, :].astype(jnp.float32)
    two[0] = total.astype(jnp.bfloat16)


def body(fronts, omega, leaf_sizes, leaf_map, own_one, parent_count, parent_map, own_two):
    _, rows, depth = fronts.shape
    cols = omega.shape[2]
    block = own_one.shape[1]
    n_row = rows // block
    params = pltpu.CompilerParams(vmem_limit_bytes=LIMIT)
    vmem, smem = whole(pltpu.VMEM), whole(pltpu.SMEM)
    near = lambda array: pltpu.with_memory_space_constraint(array, pltpu.VMEM)
    blank = pl.pallas_call(
        first_kernel,
        out_shape=pltpu.VMEM((CODE_ROWS, cols), jnp.float32),
        in_specs=[],
        out_specs=vmem,
        compiler_params=params,
        cost_estimate=pl.CostEstimate(flops=8 * 10**9, bytes_accessed=2**24, transcendentals=0),
        name="first",
    )()
    pick = pltpu.VMEM((2 * rows, rows), jnp.bfloat16)
    code, lower, upper = pl.pallas_call(
        index_kernel,
        out_shape=(pltpu.VMEM((CODE_ROWS, rows), jnp.bfloat16), pick, pick),
        in_specs=[vmem] * 3 + [smem, smem],
        out_specs=(vmem,) * 3,
        compiler_params=params,
        name="index",
    )(near(blank), leaf_map, parent_map, leaf_sizes, parent_count)
    message, rest, late = pl.pallas_call(
        product_kernel,
        out_shape=(
            pltpu.VMEM((rows + block + CODE_ROWS, cols), jnp.bfloat16),
            pltpu.VMEM((rows, cols), jnp.bfloat16),
            pltpu.VMEM((block, cols), jnp.bfloat16),
        ),
        in_specs=[vmem] * 5,
        out_specs=(vmem,) * 3,
        compiler_params=params,
        name="product",
    )(fronts, omega, own_one, own_two, near(code))
    both = lax.all_gather(message, "core")
    pieces = pl.pallas_call(
        place_kernel,
        out_shape=pltpu.VMEM((2 * n_row, 2 * block, cols), jnp.bfloat16),
        in_specs=[vmem] * 5,
        out_specs=vmem,
        compiler_params=params,
        name="place",
    )(near(message), near(rest), near(both), near(lower), near(upper))
    pieces = lax.all_to_all(pieces, ("row", "y"), 0, 0)
    shape = jax.ShapeDtypeStruct(own_one.shape, jnp.bfloat16)
    return pl.pallas_call(
        sum_kernel,
        out_shape=(shape, shape),
        in_specs=[vmem, vmem, vmem],
        out_specs=(vmem, vmem),
        compiler_params=params,
        name="total",
    )(near(pieces), near(message), near(late))


def solution(mesh):
    n_cube, n_row = mesh.devices.shape
    grouped = Mesh(mesh.devices.reshape(n_cube // 4, 2, 2, n_row), ("group", "y", "core", "row"))
    cube = ("group", "y", "core")
    in_specs = (
        P(cube, None, "row"),
        P(cube, "row", None),
        P(cube),
        P(cube, None),
        P(cube, "row", None),
        P(cube),
        P(cube, None),
        P(cube, "row", None),
    )
    out_specs = (P(cube, "row", None), P(cube, "row", None))
    return jax.shard_map(body, mesh=grouped, in_specs=in_specs, out_specs=out_specs, check_vma=False)
```

```python
import jax
import jax.numpy as jnp
from jax import lax
from jax.experimental import pallas as pl
from jax.experimental.pallas import tpu as pltpu
from jax.sharding import Mesh, PartitionSpec as P

DIGIT = 32
CODE_ROWS = 16
LIMIT = 32 * 2**20


def whole(memory):
    return pl.BlockSpec(memory_space=memory)


def picks(blocks, index):
    rows = index.shape[1]
    line = lax.broadcasted_iota(jnp.int32, (rows, rows), 0)
    return jnp.concatenate([(line + block * rows == index).astype(jnp.bfloat16) for block in blocks], axis=0)


def first_kernel(out):
    out[...] = jnp.zeros_like(out)


def index_kernel(blank, leaf_map, parent_map, leaf_size, count, code, lower):
    rows = leaf_map.shape[1]
    core = lax.axis_index("core")
    place = lax.broadcasted_iota(jnp.int32, (1, rows), 1)
    leaf = jnp.where(place < leaf_size[0], leaf_map[...], -1)
    parent = jnp.where(place < count[0], parent_map[...], -1)
    line = lax.broadcasted_iota(jnp.int32, (CODE_ROWS, rows), 0)
    digits = jnp.where(line < 2, leaf, parent)
    digits = jnp.where(line % 2 == 0, digits >> 5, digits & (DIGIT - 1))
    code[...] = (digits.astype(jnp.float32) + blank[...]).astype(jnp.bfloat16)
    lower[...] = picks((core, 1 - core), leaf)


def product_kernel(fronts, omega, own_one, own_two, code, out, rest, two):
    rows = fronts.shape[1]
    mine = own_one.shape[1]
    out[rows : rows + mine, :] = own_one[0]
    out[rows + mine :, :] = code[...]
    two[...] = own_two[0]
    partial = jnp.dot(fronts[0], omega[0], preferred_element_type=jnp.float32)
    high = partial.astype(jnp.bfloat16)
    out[:rows, :] = high
    rest[...] = (partial - high.astype(jnp.float32)).astype(jnp.bfloat16)


def decode(code):
    digits = code.astype(jnp.float32)
    leaf = digits[0:1] * DIGIT + digits[1:2]
    parent = digits[2:3] * DIGIT + digits[3:4]
    return leaf.astype(jnp.int32), parent.astype(jnp.int32)


def place_kernel(mine, rest, both, lower, out):
    rows = out.shape[2]
    block = out.shape[1] // 2
    n_row = rows // block
    core, row, here = lax.axis_index("core"), lax.axis_index("row"), lax.axis_index("y")
    other = both.at[1 - core]
    codes = mine[rows + block :, :], other[rows + block :, :]
    (leaf, parent), (other_leaf, other_parent) = decode(codes[0]), decode(codes[1])
    other_lower = picks((core, 1 - core), other_leaf)
    table = jnp.concatenate(codes, axis=1)
    targets = []
    for index, pick in ((leaf, lower[...]), (other_leaf, other_lower)):
        _, target = decode(jnp.dot(table, pick, preferred_element_type=jnp.float32))
        targets.append(jnp.where(index >= 0, target, -1))
    own = []
    for index in (parent, other_parent):
        turned = pltpu.roll(jnp.broadcast_to(index, (8, rows)), lax.rem(n_row - row, n_row) * block, 1)
        own.append(turned[:1, :block])
    own = jnp.concatenate(own, axis=1)
    line = lax.broadcasted_iota(jnp.int32, (rows, 2 * block), 0)
    partial = jnp.concatenate([mine[:rows, :], rest[...], other[:rows, :]], axis=0)
    pick = jnp.concatenate([lower[:rows], lower[:rows], other_lower[:rows]], axis=1)
    level_one = jnp.dot(pick, partial, preferred_element_type=jnp.float32).astype(jnp.bfloat16)
    for x in range(n_row):
        out[2 * x + here, block:, :] = level_one[x * block : (x + 1) * block]
    partial = jnp.concatenate([partial, mine[rows : rows + block, :], other[rows : rows + block, :]], axis=0)
    for k, y in enumerate((here, 1 - here)):
        quarter = core + 2 * y
        picked = picks((quarter,), targets[0])
        pick = [picked, picked, picks((quarter,), targets[1]), (line + quarter * rows == own).astype(jnp.bfloat16)]
        placed = jnp.dot(jnp.concatenate(pick, axis=1), partial, preferred_element_type=jnp.float32)
        high = placed.astype(jnp.bfloat16)
        for x in range(n_row):
            out[2 * x + y, :block, :] = high[x * block : (x + 1) * block]
        if k == 1:
            low = (placed - high.astype(jnp.float32)).astype(jnp.bfloat16)
            for x in range(n_row):
                out[2 * x + y, block:, :] = low[x * block : (x + 1) * block]


def sum_kernel(pieces, message, own_two, one, two):
    n_row, rows = pieces.shape[0] // 2, pieces.shape[2]
    block = own_two.shape[0]
    y = lax.axis_index("y")
    total = message[rows : rows + block, :].astype(jnp.float32)
    for x in range(n_row):
        total += pieces[2 * x + y, block:, :].astype(jnp.float32)
    one[0] = total.astype(jnp.bfloat16)
    total = own_two[...].astype(jnp.float32)
    for k in range(2 * n_row):
        total += pieces[k, :block, :].astype(jnp.float32)
    for x in range(n_row):
        total += pieces[2 * x + 1 - y, block:, :].astype(jnp.float32)
    two[0] = total.astype(jnp.bfloat16)


def body(fronts, omega, leaf_sizes, leaf_map, own_one, parent_count, parent_map, own_two):
    _, rows, depth = fronts.shape
    cols = omega.shape[2]
    block = own_one.shape[1]
    n_row = rows // block
    params = pltpu.CompilerParams(vmem_limit_bytes=LIMIT)
    vmem, smem = whole(pltpu.VMEM), whole(pltpu.SMEM)
    near = lambda array: pltpu.with_memory_space_constraint(array, pltpu.VMEM)
    blank = pl.pallas_call(
        first_kernel,
        out_shape=pltpu.VMEM((CODE_ROWS, cols), jnp.float32),
        in_specs=[],
        out_specs=vmem,
        compiler_params=params,
        cost_estimate=pl.CostEstimate(flops=8 * 10**9, bytes_accessed=2**24, transcendentals=0),
        name="first",
    )()
    pick = pltpu.VMEM((2 * rows, rows), jnp.bfloat16)
    code, lower = pl.pallas_call(
        index_kernel,
        out_shape=(pltpu.VMEM((CODE_ROWS, rows), jnp.bfloat16), pick),
        in_specs=[vmem] * 3 + [smem, smem],
        out_specs=(vmem,) * 2,
        compiler_params=params,
        name="index",
    )(near(blank), leaf_map, parent_map, leaf_sizes, parent_count)
    message, rest, late = pl.pallas_call(
        product_kernel,
        out_shape=(
            pltpu.VMEM((rows + block + CODE_ROWS, cols), jnp.bfloat16),
            pltpu.VMEM((rows, cols), jnp.bfloat16),
            pltpu.VMEM((block, cols), jnp.bfloat16),
        ),
        in_specs=[vmem] * 5,
        out_specs=(vmem,) * 3,
        compiler_params=params,
        name="product",
    )(fronts, omega, own_one, own_two, near(code))
    both = lax.all_gather(message, "core")
    pieces = pl.pallas_call(
        place_kernel,
        out_shape=pltpu.VMEM((2 * n_row, 2 * block, cols), jnp.bfloat16),
        in_specs=[vmem] * 4,
        out_specs=vmem,
        compiler_params=params,
        name="place",
    )(near(message), near(rest), near(both), near(lower))
    pieces = lax.all_to_all(pieces, ("row", "y"), 0, 0)
    shape = jax.ShapeDtypeStruct(own_one.shape, jnp.bfloat16)
    return pl.pallas_call(
        sum_kernel,
        out_shape=(shape, shape),
        in_specs=[vmem, vmem, vmem],
        out_specs=(vmem, vmem),
        compiler_params=params,
        name="total",
    )(near(pieces), near(message), near(late))


def solution(mesh):
    n_cube, n_row = mesh.devices.shape
    grouped = Mesh(mesh.devices.reshape(n_cube // 4, 2, 2, n_row), ("group", "y", "core", "row"))
    cube = ("group", "y", "core")
    in_specs = (
        P(cube, None, "row"),
        P(cube, "row", None),
        P(cube),
        P(cube, None),
        P(cube, "row", None),
        P(cube),
        P(cube, None),
        P(cube, "row", None),
    )
    out_specs = (P(cube, "row", None), P(cube, "row", None))
    return jax.shard_map(body, mesh=grouped, in_specs=in_specs, out_specs=out_specs, check_vma=False)
```

```python
import jax
import jax.numpy as jnp
from jax import lax
from jax.experimental import pallas as pl
from jax.experimental.pallas import tpu as pltpu
from jax.sharding import Mesh, PartitionSpec as P

DIGIT = 32
LANES = 128
CODE_ROWS = 16
LIMIT = 32 * 2**20


def whole(memory):
    return pl.BlockSpec(memory_space=memory)


def picks(blocks, index):
    rows = index.shape[1]
    line = lax.broadcasted_iota(jnp.int32, (rows, rows), 0)
    return jnp.concatenate([(line + block * rows == index).astype(jnp.bfloat16) for block in blocks], axis=0)


def first_kernel(out):
    out[...] = jnp.zeros_like(out)


def index_kernel(blank, leaf_map, parent_map, leaf_size, count, code, lower):
    rows = leaf_map.shape[1]
    core = lax.axis_index("core")
    place = lax.broadcasted_iota(jnp.int32, (1, rows), 1)
    leaf = jnp.where(place < leaf_size[0], leaf_map[...], -1)
    parent = jnp.where(place < count[0], parent_map[...], -1)
    line = lax.broadcasted_iota(jnp.int32, (CODE_ROWS, rows), 0)
    digits = jnp.where(line < 2, leaf, parent)
    digits = jnp.where(line % 2 == 0, digits >> 5, digits & (DIGIT - 1))
    code[...] = (digits.astype(jnp.float32) + blank[...]).astype(jnp.bfloat16)
    lower[...] = picks((core,), leaf)


def product_kernel(fronts, omega, own_one, own_two, code, out, rest, two):
    rows = fronts.shape[1]
    mine = own_one.shape[1]
    out[rows : rows + mine, :] = own_one[0]
    out[rows + mine :, :] = code[...]
    two[...] = own_two[0]
    partial = jnp.dot(fronts[0], omega[0], preferred_element_type=jnp.float32)
    high = partial.astype(jnp.bfloat16)
    out[:rows, :] = high
    rest[...] = (partial - high.astype(jnp.float32)).astype(jnp.bfloat16)


def decode(code):
    digits = code.astype(jnp.float32)
    leaf = digits[0:1] * DIGIT + digits[1:2]
    parent = digits[2:3] * DIGIT + digits[3:4]
    return leaf.astype(jnp.int32), parent.astype(jnp.int32)


def place_kernel(mine, rest, both, lower, out):
    rows = out.shape[2]
    block = out.shape[1] // 2
    n_row = rows // block
    core, row, here = lax.axis_index("core"), lax.axis_index("row"), lax.axis_index("y")
    other = both.at[1 - core]
    leaf, parent = decode(mine[rows + block :, :])
    other_leaf, other_parent = decode(other[rows + block :, :])
    other_lower = picks((core,), other_leaf)
    pages = [jnp.broadcast_to(half[:, k : k + LANES], (8, LANES)) for half in (parent, other_parent) for k in range(0, rows, LANES)]
    targets = []
    for index in (leaf, other_leaf):
        found = []
        for k in range(0, rows, LANES):
            at = jnp.broadcast_to(jnp.bitwise_xor(index[:, k : k + LANES], core * rows), (8, LANES))
            value = jnp.full((8, LANES), -1, jnp.int32)
            for page, entries in enumerate(pages):
                entry = jnp.take_along_axis(entries, at & (LANES - 1), axis=1, mode="promise_in_bounds")
                value = jnp.where(at >> 7 == page, entry, value)
            found.append(value[:1])
        targets.append(jnp.concatenate(found, axis=1))
    own = []
    for index in (parent, other_parent):
        turned = pltpu.roll(jnp.broadcast_to(index, (8, rows)), lax.rem(n_row - row, n_row) * block, 1)
        own.append(turned[:1, :block])
    own = jnp.concatenate(own, axis=1)
    line = lax.broadcasted_iota(jnp.int32, (rows, 2 * block), 0)
    partial = jnp.concatenate([mine[:rows, :], rest[...], other[:rows, :]], axis=0)
    pick = jnp.concatenate([lower[...], lower[...], other_lower], axis=1)
    level_one = jnp.dot(pick, partial, preferred_element_type=jnp.float32).astype(jnp.bfloat16)
    for x in range(n_row):
        out[2 * x + here, block:, :] = level_one[x * block : (x + 1) * block]
    partial = jnp.concatenate([partial, mine[rows : rows + block, :], other[rows : rows + block, :]], axis=0)
    for k, y in enumerate((here, 1 - here)):
        quarter = core + 2 * y
        picked = picks((quarter,), targets[0])
        pick = [picked, picked, picks((quarter,), targets[1]), (line + quarter * rows == own).astype(jnp.bfloat16)]
        placed = jnp.dot(jnp.concatenate(pick, axis=1), partial, preferred_element_type=jnp.float32)
        high = placed.astype(jnp.bfloat16)
        for x in range(n_row):
            out[2 * x + y, :block, :] = high[x * block : (x + 1) * block]
        if k == 1:
            low = (placed - high.astype(jnp.float32)).astype(jnp.bfloat16)
            for x in range(n_row):
                out[2 * x + y, block:, :] = low[x * block : (x + 1) * block]


def sum_kernel(pieces, message, own_two, one, two):
    n_row, rows = pieces.shape[0] // 2, pieces.shape[2]
    block = own_two.shape[0]
    y = lax.axis_index("y")
    total = message[rows : rows + block, :].astype(jnp.float32)
    for x in range(n_row):
        total += pieces[2 * x + y, block:, :].astype(jnp.float32)
    one[0] = total.astype(jnp.bfloat16)
    total = own_two[...].astype(jnp.float32)
    for k in range(2 * n_row):
        total += pieces[k, :block, :].astype(jnp.float32)
    for x in range(n_row):
        total += pieces[2 * x + 1 - y, block:, :].astype(jnp.float32)
    two[0] = total.astype(jnp.bfloat16)


def body(fronts, omega, leaf_sizes, leaf_map, own_one, parent_count, parent_map, own_two):
    _, rows, depth = fronts.shape
    cols = omega.shape[2]
    block = own_one.shape[1]
    n_row = rows // block
    params = pltpu.CompilerParams(vmem_limit_bytes=LIMIT)
    vmem, smem = whole(pltpu.VMEM), whole(pltpu.SMEM)
    near = lambda array: pltpu.with_memory_space_constraint(array, pltpu.VMEM)
    blank = pl.pallas_call(
        first_kernel,
        out_shape=pltpu.VMEM((CODE_ROWS, cols), jnp.float32),
        in_specs=[],
        out_specs=vmem,
        compiler_params=params,
        cost_estimate=pl.CostEstimate(flops=8 * 10**9, bytes_accessed=2**24, transcendentals=0),
        name="first",
    )()
    pick = pltpu.VMEM((rows, rows), jnp.bfloat16)
    code, lower = pl.pallas_call(
        index_kernel,
        out_shape=(pltpu.VMEM((CODE_ROWS, rows), jnp.bfloat16), pick),
        in_specs=[vmem] * 3 + [smem, smem],
        out_specs=(vmem,) * 2,
        compiler_params=params,
        name="index",
    )(near(blank), leaf_map, parent_map, leaf_sizes, parent_count)
    message, rest, late = pl.pallas_call(
        product_kernel,
        out_shape=(
            pltpu.VMEM((rows + block + CODE_ROWS, cols), jnp.bfloat16),
            pltpu.VMEM((rows, cols), jnp.bfloat16),
            pltpu.VMEM((block, cols), jnp.bfloat16),
        ),
        in_specs=[vmem] * 5,
        out_specs=(vmem,) * 3,
        compiler_params=params,
        name="product",
    )(fronts, omega, own_one, own_two, near(code))
    both = lax.all_gather(message, "core")
    pieces = pl.pallas_call(
        place_kernel,
        out_shape=pltpu.VMEM((2 * n_row, 2 * block, cols), jnp.bfloat16),
        in_specs=[vmem] * 4,
        out_specs=vmem,
        compiler_params=params,
        name="place",
    )(near(message), near(rest), near(both), near(lower))
    pieces = lax.all_to_all(pieces, ("row", "y"), 0, 0)
    shape = jax.ShapeDtypeStruct(own_one.shape, jnp.bfloat16)
    return pl.pallas_call(
        sum_kernel,
        out_shape=(shape, shape),
        in_specs=[vmem, vmem, vmem],
        out_specs=(vmem, vmem),
        compiler_params=params,
        name="total",
    )(near(pieces), near(message), near(late))


def solution(mesh):
    n_cube, n_row = mesh.devices.shape
    grouped = Mesh(mesh.devices.reshape(n_cube // 4, 2, 2, n_row), ("group", "y", "core", "row"))
    cube = ("group", "y", "core")
    in_specs = (
        P(cube, None, "row"),
        P(cube, "row", None),
        P(cube),
        P(cube, None),
        P(cube, "row", None),
        P(cube),
        P(cube, None),
        P(cube, "row", None),
    )
    out_specs = (P(cube, "row", None), P(cube, "row", None))
    return jax.shard_map(body, mesh=grouped, in_specs=in_specs, out_specs=out_specs, check_vma=False)
```

```python
import jax
import jax.numpy as jnp
from jax import lax
from jax.experimental import pallas as pl
from jax.experimental.pallas import tpu as pltpu
from jax.sharding import Mesh, PartitionSpec as P

DIGIT = 32
LANES = 128
TIER = 64
CODE_ROWS = 16
LIMIT = 32 * 2**20


def whole(memory):
    return pl.BlockSpec(memory_space=memory)


def picks(blocks, index):
    rows = index.shape[1]
    line = lax.broadcasted_iota(jnp.int32, (rows, rows), 0)
    return jnp.concatenate([(line + block * rows == index).astype(jnp.bfloat16) for block in blocks], axis=0)


def first_kernel(out):
    out[...] = jnp.zeros_like(out)


def index_kernel(blank, leaf_map, parent_map, leaf_size, count, code, lower):
    rows = leaf_map.shape[1]
    core = lax.axis_index("core")
    place = lax.broadcasted_iota(jnp.int32, (1, rows), 1)
    leaf = jnp.where(place < leaf_size[0], leaf_map[...], -1)
    parent = jnp.where(place < count[0], parent_map[...], -1)
    line = lax.broadcasted_iota(jnp.int32, (CODE_ROWS, rows), 0)
    digits = jnp.where(line < 2, leaf, parent)
    digits = jnp.where(line % 2 == 0, digits >> 5, digits & (DIGIT - 1))
    code[...] = (digits.astype(jnp.float32) + blank[...]).astype(jnp.bfloat16)
    lower[...] = picks((core,), leaf)


def product_kernel(fronts, omega, own_one, own_two, code, leaf_size, out, rest, two):
    rows = fronts.shape[1]
    mine = own_one.shape[1]
    out[rows : rows + mine, :] = own_one[0]
    out[rows + mine :, :] = code[...]
    two[...] = own_two[0]

    def multiply(live):
        partial = jnp.dot(fronts[0, :live, :], omega[0], preferred_element_type=jnp.float32)
        high = partial.astype(jnp.bfloat16)
        out[:live, :] = high
        rest[:live, :] = (partial - high.astype(jnp.float32)).astype(jnp.bfloat16)
        if live < rows:
            dead = jnp.zeros((rows - live, out.shape[1]), jnp.bfloat16)
            out[live:rows, :] = dead
            rest[live:, :] = dead

    size = leaf_size[0]
    for live in range(2 * TIER, rows + 1, TIER):
        above = live - TIER if live > 2 * TIER else -1
        wanted = size <= live if live < rows else size > above
        pl.when(jnp.logical_and(size > above, wanted))(lambda live=live: multiply(live))


def decode(code):
    digits = code.astype(jnp.float32)
    leaf = digits[0:1] * DIGIT + digits[1:2]
    parent = digits[2:3] * DIGIT + digits[3:4]
    return leaf.astype(jnp.int32), parent.astype(jnp.int32)


def place_kernel(mine, rest, both, lower, out):
    rows = out.shape[2]
    block = out.shape[1] // 2
    n_row = rows // block
    core, row, here = lax.axis_index("core"), lax.axis_index("row"), lax.axis_index("y")
    other = both.at[1 - core]
    leaf, parent = decode(mine[rows + block :, :])
    other_leaf, other_parent = decode(other[rows + block :, :])
    other_lower = picks((core,), other_leaf)
    pages = [jnp.broadcast_to(half[:, k : k + LANES], (8, LANES)) for half in (parent, other_parent) for k in range(0, rows, LANES)]
    targets = []
    for index in (leaf, other_leaf):
        found = []
        for k in range(0, rows, LANES):
            at = jnp.broadcast_to(jnp.bitwise_xor(index[:, k : k + LANES], core * rows), (8, LANES))
            value = jnp.full((8, LANES), -1, jnp.int32)
            for page, entries in enumerate(pages):
                entry = jnp.take_along_axis(entries, at & (LANES - 1), axis=1, mode="promise_in_bounds")
                value = jnp.where(at >> 7 == page, entry, value)
            found.append(value[:1])
        targets.append(jnp.concatenate(found, axis=1))
    own = []
    for index in (parent, other_parent):
        turned = pltpu.roll(jnp.broadcast_to(index, (8, rows)), lax.rem(n_row - row, n_row) * block, 1)
        own.append(turned[:1, :block])
    own = jnp.concatenate(own, axis=1)
    line = lax.broadcasted_iota(jnp.int32, (rows, 2 * block), 0)
    partial = jnp.concatenate([mine[:rows, :], rest[...], other[:rows, :]], axis=0)
    pick = jnp.concatenate([lower[...], lower[...], other_lower], axis=1)
    level_one = jnp.dot(pick, partial, preferred_element_type=jnp.float32).astype(jnp.bfloat16)
    for x in range(n_row):
        out[2 * x + here, block:, :] = level_one[x * block : (x + 1) * block]
    partial = jnp.concatenate([partial, mine[rows : rows + block, :], other[rows : rows + block, :]], axis=0)
    for k, y in enumerate((here, 1 - here)):
        quarter = core + 2 * y
        picked = picks((quarter,), targets[0])
        pick = [picked, picked, picks((quarter,), targets[1]), (line + quarter * rows == own).astype(jnp.bfloat16)]
        placed = jnp.dot(jnp.concatenate(pick, axis=1), partial, preferred_element_type=jnp.float32)
        high = placed.astype(jnp.bfloat16)
        for x in range(n_row):
            out[2 * x + y, :block, :] = high[x * block : (x + 1) * block]
        if k == 1:
            low = (placed - high.astype(jnp.float32)).astype(jnp.bfloat16)
            for x in range(n_row):
                out[2 * x + y, block:, :] = low[x * block : (x + 1) * block]


def sum_kernel(pieces, message, own_two, one, two):
    n_row, rows = pieces.shape[0] // 2, pieces.shape[2]
    block = own_two.shape[0]
    y = lax.axis_index("y")
    total = message[rows : rows + block, :].astype(jnp.float32)
    for x in range(n_row):
        total += pieces[2 * x + y, block:, :].astype(jnp.float32)
    one[0] = total.astype(jnp.bfloat16)
    total = own_two[...].astype(jnp.float32)
    for k in range(2 * n_row):
        total += pieces[k, :block, :].astype(jnp.float32)
    for x in range(n_row):
        total += pieces[2 * x + 1 - y, block:, :].astype(jnp.float32)
    two[0] = total.astype(jnp.bfloat16)


def body(fronts, omega, leaf_sizes, leaf_map, own_one, parent_count, parent_map, own_two):
    _, rows, depth = fronts.shape
    cols = omega.shape[2]
    block = own_one.shape[1]
    n_row = rows // block
    params = pltpu.CompilerParams(vmem_limit_bytes=LIMIT)
    vmem, smem = whole(pltpu.VMEM), whole(pltpu.SMEM)
    near = lambda array: pltpu.with_memory_space_constraint(array, pltpu.VMEM)
    blank = pl.pallas_call(
        first_kernel,
        out_shape=pltpu.VMEM((CODE_ROWS, cols), jnp.float32),
        in_specs=[],
        out_specs=vmem,
        compiler_params=params,
        cost_estimate=pl.CostEstimate(flops=8 * 10**9, bytes_accessed=2**24, transcendentals=0),
        name="first",
    )()
    pick = pltpu.VMEM((rows, rows), jnp.bfloat16)
    code, lower = pl.pallas_call(
        index_kernel,
        out_shape=(pltpu.VMEM((CODE_ROWS, rows), jnp.bfloat16), pick),
        in_specs=[vmem] * 3 + [smem, smem],
        out_specs=(vmem,) * 2,
        compiler_params=params,
        name="index",
    )(near(blank), leaf_map, parent_map, leaf_sizes, parent_count)
    message, rest, late = pl.pallas_call(
        product_kernel,
        out_shape=(
            pltpu.VMEM((rows + block + CODE_ROWS, cols), jnp.bfloat16),
            pltpu.VMEM((rows, cols), jnp.bfloat16),
            pltpu.VMEM((block, cols), jnp.bfloat16),
        ),
        in_specs=[vmem] * 5 + [smem],
        out_specs=(vmem,) * 3,
        compiler_params=params,
        name="product",
    )(fronts, omega, own_one, own_two, near(code), leaf_sizes)
    both = lax.all_gather(message, "core")
    pieces = pl.pallas_call(
        place_kernel,
        out_shape=pltpu.VMEM((2 * n_row, 2 * block, cols), jnp.bfloat16),
        in_specs=[vmem] * 4,
        out_specs=vmem,
        compiler_params=params,
        name="place",
    )(near(message), near(rest), near(both), near(lower))
    pieces = lax.all_to_all(pieces, ("row", "y"), 0, 0)
    shape = jax.ShapeDtypeStruct(own_one.shape, jnp.bfloat16)
    return pl.pallas_call(
        sum_kernel,
        out_shape=(shape, shape),
        in_specs=[vmem, vmem, vmem],
        out_specs=(vmem, vmem),
        compiler_params=params,
        name="total",
    )(near(pieces), near(message), near(late))


def solution(mesh):
    n_cube, n_row = mesh.devices.shape
    grouped = Mesh(mesh.devices.reshape(n_cube // 4, 2, 2, n_row), ("group", "y", "core", "row"))
    cube = ("group", "y", "core")
    in_specs = (
        P(cube, None, "row"),
        P(cube, "row", None),
        P(cube),
        P(cube, None),
        P(cube, "row", None),
        P(cube),
        P(cube, None),
        P(cube, "row", None),
    )
    out_specs = (P(cube, "row", None), P(cube, "row", None))
    return jax.shard_map(body, mesh=grouped, in_specs=in_specs, out_specs=out_specs, check_vma=False)
```

```python
import jax
import jax.numpy as jnp
from jax import lax
from jax.experimental import pallas as pl
from jax.experimental.pallas import tpu as pltpu
from jax.sharding import Mesh, PartitionSpec as P

DIGIT = 32
LANES = 128
TIER = 64
CODE_ROWS = 16
LIMIT = 32 * 2**20


def whole(memory):
    return pl.BlockSpec(memory_space=memory)


def picks(blocks, index):
    rows = index.shape[1]
    line = lax.broadcasted_iota(jnp.int32, (rows, rows), 0)
    return jnp.concatenate([(line + block * rows == index).astype(jnp.bfloat16) for block in blocks], axis=0)


def first_kernel(out):
    out[...] = jnp.zeros_like(out)


def index_kernel(blank, leaf_map, parent_map, leaf_size, count, code, lower):
    rows = leaf_map.shape[1]
    core = lax.axis_index("core")
    place = lax.broadcasted_iota(jnp.int32, (1, rows), 1)
    leaf = jnp.where(place < leaf_size[0], leaf_map[...], -1)
    parent = jnp.where(place < count[0], parent_map[...], -1)
    line = lax.broadcasted_iota(jnp.int32, (CODE_ROWS, rows), 0)
    digits = jnp.where(line < 2, leaf, parent)
    digits = jnp.where(line % 2 == 0, digits >> 5, digits & (DIGIT - 1))
    code[...] = (digits.astype(jnp.float32) + blank[...]).astype(jnp.bfloat16)
    lower[...] = picks((core,), leaf)


def product_kernel(fronts, omega, own_one, own_two, code, leaf_size, out, rest, two):
    rows = fronts.shape[1]
    mine = own_one.shape[1]
    out[rows : rows + mine, :] = own_one[0]
    out[rows + mine :, :] = code[...]
    two[...] = own_two[0]

    def multiply(live):
        partial = jnp.dot(fronts[0, :live, :], omega[0], preferred_element_type=jnp.float32)
        high = partial.astype(jnp.bfloat16)
        out[:live, :] = high
        rest[:live, :] = (partial - high.astype(jnp.float32)).astype(jnp.bfloat16)
        if live < rows:
            dead = jnp.zeros((rows - live, out.shape[1]), jnp.bfloat16)
            out[live:rows, :] = dead
            rest[live:, :] = dead

    size = leaf_size[0]
    for live in range(2 * TIER, rows + 1, TIER):
        above = live - TIER if live > 2 * TIER else -1
        wanted = size <= live if live < rows else size > above
        pl.when(jnp.logical_and(size > above, wanted))(lambda live=live: multiply(live))


def decode(code):
    digits = code.astype(jnp.float32)
    leaf = digits[0:1] * DIGIT + digits[1:2]
    parent = digits[2:3] * DIGIT + digits[3:4]
    return leaf.astype(jnp.int32), parent.astype(jnp.int32)


def place_kernel(mine, rest, both, lower, out):
    rows = out.shape[2]
    block = out.shape[1] // 2
    n_row = rows // block
    core, row, here = lax.axis_index("core"), lax.axis_index("row"), lax.axis_index("y")
    other = both.at[1 - core]
    leaf, parent = decode(mine[rows + block :, :])
    other_leaf, other_parent = decode(other[rows + block :, :])
    other_lower = picks((core,), other_leaf)
    pages = [jnp.broadcast_to(half[:, k : k + LANES], (8, LANES)) for half in (parent, other_parent) for k in range(0, rows, LANES)]
    targets = []
    for index in (leaf, other_leaf):
        found = []
        for k in range(0, rows, LANES):
            at = jnp.broadcast_to(jnp.bitwise_xor(index[:, k : k + LANES], core * rows), (8, LANES))
            value = jnp.full((8, LANES), -1, jnp.int32)
            for page, entries in enumerate(pages):
                entry = jnp.take_along_axis(entries, at & (LANES - 1), axis=1, mode="promise_in_bounds")
                value = jnp.where(at >> 7 == page, entry, value)
            found.append(value[:1])
        targets.append(jnp.concatenate(found, axis=1))
    own = []
    for index in (parent, other_parent):
        turned = pltpu.roll(jnp.broadcast_to(index, (8, rows)), lax.rem(n_row - row, n_row) * block, 1)
        own.append(turned[:1, :block])
    own = jnp.concatenate(own, axis=1)
    line = lax.broadcasted_iota(jnp.int32, (rows, 2 * block), 0)
    partial = jnp.concatenate([mine[:rows, :], rest[...], other[:rows, :]], axis=0)
    pick = jnp.concatenate([lower[...], lower[...], other_lower], axis=1)
    level_one = jnp.dot(pick, partial, preferred_element_type=jnp.float32).astype(jnp.bfloat16)
    for x in range(n_row):
        out[2 * x + here, block:, :] = level_one[x * block : (x + 1) * block]
    partial = jnp.concatenate([partial, mine[rows : rows + block, :], other[rows : rows + block, :]], axis=0)
    for k, y in enumerate((1 - here, here)):
        quarter = core + 2 * y
        picked = picks((quarter,), targets[0])
        pick = [picked, picked, picks((quarter,), targets[1]), (line + quarter * rows == own).astype(jnp.bfloat16)]
        placed = jnp.dot(jnp.concatenate(pick, axis=1), partial, preferred_element_type=jnp.float32)
        high = placed.astype(jnp.bfloat16)
        for x in range(n_row):
            out[2 * x + y, :block, :] = high[x * block : (x + 1) * block]
        if k == 0:
            low = (placed - high.astype(jnp.float32)).astype(jnp.bfloat16)
            for x in range(n_row):
                out[2 * x + y, block:, :] = low[x * block : (x + 1) * block]


def sum_kernel(pieces, message, own_two, one, two):
    n_row, rows = pieces.shape[0] // 2, pieces.shape[2]
    block = own_two.shape[0]
    y = lax.axis_index("y")
    total = message[rows : rows + block, :].astype(jnp.float32)
    for x in range(n_row):
        total += pieces[2 * x + y, block:, :].astype(jnp.float32)
    one[0] = total.astype(jnp.bfloat16)
    total = own_two[...].astype(jnp.float32)
    for k in range(2 * n_row):
        total += pieces[k, :block, :].astype(jnp.float32)
    for x in range(n_row):
        total += pieces[2 * x + 1 - y, block:, :].astype(jnp.float32)
    two[0] = total.astype(jnp.bfloat16)


def body(fronts, omega, leaf_sizes, leaf_map, own_one, parent_count, parent_map, own_two):
    _, rows, depth = fronts.shape
    cols = omega.shape[2]
    block = own_one.shape[1]
    n_row = rows // block
    params = pltpu.CompilerParams(vmem_limit_bytes=LIMIT)
    vmem, smem = whole(pltpu.VMEM), whole(pltpu.SMEM)
    near = lambda array: pltpu.with_memory_space_constraint(array, pltpu.VMEM)
    blank = pl.pallas_call(
        first_kernel,
        out_shape=pltpu.VMEM((CODE_ROWS, cols), jnp.float32),
        in_specs=[],
        out_specs=vmem,
        compiler_params=params,
        cost_estimate=pl.CostEstimate(flops=8 * 10**9, bytes_accessed=2**24, transcendentals=0),
        name="first",
    )()
    pick = pltpu.VMEM((rows, rows), jnp.bfloat16)
    code, lower = pl.pallas_call(
        index_kernel,
        out_shape=(pltpu.VMEM((CODE_ROWS, rows), jnp.bfloat16), pick),
        in_specs=[vmem] * 3 + [smem, smem],
        out_specs=(vmem,) * 2,
        compiler_params=params,
        name="index",
    )(near(blank), leaf_map, parent_map, leaf_sizes, parent_count)
    message, rest, late = pl.pallas_call(
        product_kernel,
        out_shape=(
            pltpu.VMEM((rows + block + CODE_ROWS, cols), jnp.bfloat16),
            pltpu.VMEM((rows, cols), jnp.bfloat16),
            pltpu.VMEM((block, cols), jnp.bfloat16),
        ),
        in_specs=[vmem] * 5 + [smem],
        out_specs=(vmem,) * 3,
        compiler_params=params,
        name="product",
    )(fronts, omega, own_one, own_two, near(code), leaf_sizes)
    both = lax.all_gather(message, "core")
    pieces = pl.pallas_call(
        place_kernel,
        out_shape=pltpu.VMEM((2 * n_row, 2 * block, cols), jnp.bfloat16),
        in_specs=[vmem] * 4,
        out_specs=vmem,
        compiler_params=params,
        name="place",
    )(near(message), near(rest), near(both), near(lower))
    pieces = lax.all_to_all(pieces, ("row", "y"), 0, 0)
    shape = jax.ShapeDtypeStruct(own_one.shape, jnp.bfloat16)
    return pl.pallas_call(
        sum_kernel,
        out_shape=(shape, shape),
        in_specs=[vmem, vmem, vmem],
        out_specs=(vmem, vmem),
        compiler_params=params,
        name="total",
    )(near(pieces), near(message), near(late))


def solution(mesh):
    n_cube, n_row = mesh.devices.shape
    grouped = Mesh(mesh.devices.reshape(n_cube // 4, 2, 2, n_row), ("group", "y", "core", "row"))
    cube = ("group", "y", "core")
    in_specs = (
        P(cube, None, "row"),
        P(cube, "row", None),
        P(cube),
        P(cube, None),
        P(cube, "row", None),
        P(cube),
        P(cube, None),
        P(cube, "row", None),
    )
    out_specs = (P(cube, "row", None), P(cube, "row", None))
    return jax.shard_map(body, mesh=grouped, in_specs=in_specs, out_specs=out_specs, check_vma=False)
```

```python
import jax
import jax.numpy as jnp
from jax import lax
from jax.experimental import pallas as pl
from jax.experimental.pallas import tpu as pltpu
from jax.sharding import Mesh, PartitionSpec as P

DIGIT = 32
LANES = 128
CODE_ROWS = 16
LIMIT = 32 * 2**20


def whole(memory):
    return pl.BlockSpec(memory_space=memory)


def picks(blocks, index):
    rows = index.shape[1]
    line = lax.broadcasted_iota(jnp.int32, (rows, rows), 0)
    return jnp.concatenate([(line + block * rows == index).astype(jnp.bfloat16) for block in blocks], axis=0)


def first_kernel(out):
    out[...] = jnp.zeros_like(out)


def index_kernel(blank, leaf_map, parent_map, leaf_size, count, code, lower):
    rows = leaf_map.shape[1]
    core = lax.axis_index("core")
    place = lax.broadcasted_iota(jnp.int32, (1, rows), 1)
    leaf = jnp.where(place < leaf_size[0], leaf_map[...], -1)
    parent = jnp.where(place < count[0], parent_map[...], -1)
    line = lax.broadcasted_iota(jnp.int32, (CODE_ROWS, rows), 0)
    digits = jnp.where(line < 2, leaf, parent)
    digits = jnp.where(line % 2 == 0, digits >> 5, digits & (DIGIT - 1))
    code[...] = (digits.astype(jnp.float32) + blank[...]).astype(jnp.bfloat16)
    lower[...] = picks((core,), leaf)


def product_kernel(fronts, omega, own_one, own_two, code, out, rest, two):
    rows = fronts.shape[1]
    mine = own_one.shape[1]
    out[rows : rows + mine, :] = own_one[0]
    out[rows + mine :, :] = code[...]
    two[...] = own_two[0]
    partial = jnp.dot(fronts[0], omega[0], preferred_element_type=jnp.float32)
    high = partial.astype(jnp.bfloat16)
    out[:rows, :] = high
    rest[...] = (partial - high.astype(jnp.float32)).astype(jnp.bfloat16)


def decode(code):
    digits = code.astype(jnp.float32)
    leaf = digits[0:1] * DIGIT + digits[1:2]
    parent = digits[2:3] * DIGIT + digits[3:4]
    return leaf.astype(jnp.int32), parent.astype(jnp.int32)


def place_kernel(mine, rest, both, lower, out):
    rows = out.shape[2]
    block = out.shape[1] // 2
    n_row = rows // block
    core, row, here = lax.axis_index("core"), lax.axis_index("row"), lax.axis_index("y")
    other = both.at[1 - core]
    leaf, parent = decode(mine[rows + block :, :])
    other_leaf, other_parent = decode(other[rows + block :, :])
    other_lower = picks((core,), other_leaf)
    pages = [jnp.broadcast_to(half[:, k : k + LANES], (8, LANES)) for half in (parent, other_parent) for k in range(0, rows, LANES)]
    targets = []
    for index in (leaf, other_leaf):
        found = []
        for k in range(0, rows, LANES):
            at = jnp.broadcast_to(jnp.bitwise_xor(index[:, k : k + LANES], core * rows), (8, LANES))
            value = jnp.full((8, LANES), -1, jnp.int32)
            for page, entries in enumerate(pages):
                entry = jnp.take_along_axis(entries, at & (LANES - 1), axis=1, mode="promise_in_bounds")
                value = jnp.where(at >> 7 == page, entry, value)
            found.append(value[:1])
        targets.append(jnp.concatenate(found, axis=1))
    own = []
    for index in (parent, other_parent):
        turned = pltpu.roll(jnp.broadcast_to(index, (8, rows)), lax.rem(n_row - row, n_row) * block, 1)
        own.append(turned[:1, :block])
    own = jnp.concatenate(own, axis=1)
    line = lax.broadcasted_iota(jnp.int32, (rows, 2 * block), 0)
    partial = jnp.concatenate([mine[:rows, :], rest[...], other[:rows, :]], axis=0)
    pick = jnp.concatenate([lower[...], lower[...], other_lower], axis=1)
    level_one = jnp.dot(pick, partial, preferred_element_type=jnp.float32).astype(jnp.bfloat16)
    for x in range(n_row):
        out[2 * x + here, block:, :] = level_one[x * block : (x + 1) * block]
    partial = jnp.concatenate([partial, mine[rows : rows + block, :], other[rows : rows + block, :]], axis=0)
    for k, y in enumerate((1 - here, here)):
        quarter = core + 2 * y
        picked = picks((quarter,), targets[0])
        pick = [picked, picked, picks((quarter,), targets[1]), (line + quarter * rows == own).astype(jnp.bfloat16)]
        placed = jnp.dot(jnp.concatenate(pick, axis=1), partial, preferred_element_type=jnp.float32)
        high = placed.astype(jnp.bfloat16)
        for x in range(n_row):
            out[2 * x + y, :block, :] = high[x * block : (x + 1) * block]
        if k == 0:
            low = (placed - high.astype(jnp.float32)).astype(jnp.bfloat16)
            for x in range(n_row):
                out[2 * x + y, block:, :] = low[x * block : (x + 1) * block]


def sum_kernel(pieces, message, own_two, one, two):
    n_row, rows = pieces.shape[0] // 2, pieces.shape[2]
    block = own_two.shape[0]
    y = lax.axis_index("y")
    total = message[rows : rows + block, :].astype(jnp.float32)
    for x in range(n_row):
        total += pieces[2 * x + y, block:, :].astype(jnp.float32)
    one[0] = total.astype(jnp.bfloat16)
    total = own_two[...].astype(jnp.float32)
    for k in range(2 * n_row):
        total += pieces[k, :block, :].astype(jnp.float32)
    for x in range(n_row):
        total += pieces[2 * x + 1 - y, block:, :].astype(jnp.float32)
    two[0] = total.astype(jnp.bfloat16)


def body(fronts, omega, leaf_sizes, leaf_map, own_one, parent_count, parent_map, own_two):
    _, rows, depth = fronts.shape
    cols = omega.shape[2]
    block = own_one.shape[1]
    n_row = rows // block
    params = pltpu.CompilerParams(vmem_limit_bytes=LIMIT)
    vmem, smem = whole(pltpu.VMEM), whole(pltpu.SMEM)
    near = lambda array: pltpu.with_memory_space_constraint(array, pltpu.VMEM)
    blank = pl.pallas_call(
        first_kernel,
        out_shape=pltpu.VMEM((CODE_ROWS, cols), jnp.float32),
        in_specs=[],
        out_specs=vmem,
        compiler_params=params,
        cost_estimate=pl.CostEstimate(flops=8 * 10**9, bytes_accessed=2**24, transcendentals=0),
        name="first",
    )()
    pick = pltpu.VMEM((rows, rows), jnp.bfloat16)
    code, lower = pl.pallas_call(
        index_kernel,
        out_shape=(pltpu.VMEM((CODE_ROWS, rows), jnp.bfloat16), pick),
        in_specs=[vmem] * 3 + [smem, smem],
        out_specs=(vmem,) * 2,
        compiler_params=params,
        name="index",
    )(near(blank), leaf_map, parent_map, leaf_sizes, parent_count)
    message, rest, late = pl.pallas_call(
        product_kernel,
        out_shape=(
            pltpu.VMEM((rows + block + CODE_ROWS, cols), jnp.bfloat16),
            pltpu.VMEM((rows, cols), jnp.bfloat16),
            pltpu.VMEM((block, cols), jnp.bfloat16),
        ),
        in_specs=[vmem] * 5,
        out_specs=(vmem,) * 3,
        compiler_params=params,
        name="product",
    )(fronts, omega, own_one, own_two, near(code))
    both = lax.all_gather(message, "core")
    pieces = pl.pallas_call(
        place_kernel,
        out_shape=pltpu.VMEM((2 * n_row, 2 * block, cols), jnp.bfloat16),
        in_specs=[vmem] * 4,
        out_specs=vmem,
        compiler_params=params,
        name="place",
    )(near(message), near(rest), near(both), near(lower))
    pieces = lax.all_to_all(pieces, ("row", "y"), 0, 0)
    shape = jax.ShapeDtypeStruct(own_one.shape, jnp.bfloat16)
    return pl.pallas_call(
        sum_kernel,
        out_shape=(shape, shape),
        in_specs=[vmem, vmem, vmem],
        out_specs=(vmem, vmem),
        compiler_params=params,
        name="total",
    )(near(pieces), near(message), near(late))


def solution(mesh):
    n_cube, n_row = mesh.devices.shape
    grouped = Mesh(mesh.devices.reshape(n_cube // 4, 2, 2, n_row), ("group", "y", "core", "row"))
    cube = ("group", "y", "core")
    in_specs = (
        P(cube, None, "row"),
        P(cube, "row", None),
        P(cube),
        P(cube, None),
        P(cube, "row", None),
        P(cube),
        P(cube, None),
        P(cube, "row", None),
    )
    out_specs = (P(cube, "row", None), P(cube, "row", None))
    return jax.shard_map(body, mesh=grouped, in_specs=in_specs, out_specs=out_specs, check_vma=False)
```

```python
import jax
import jax.numpy as jnp
from jax import lax
from jax.experimental import pallas as pl
from jax.experimental.pallas import tpu as pltpu
from jax.sharding import Mesh, PartitionSpec as P

DIGIT = 32
LANES = 128
CODE_ROWS = 16
LIMIT = 32 * 2**20


def whole(memory):
    return pl.BlockSpec(memory_space=memory)


def picks(blocks, index):
    rows = index.shape[1]
    line = lax.broadcasted_iota(jnp.int32, (rows, rows), 0)
    return jnp.concatenate([(line + block * rows == index).astype(jnp.bfloat16) for block in blocks], axis=0)


def first_kernel(out):
    out[...] = jnp.zeros_like(out)


def index_kernel(blank, leaf_map, parent_map, leaf_size, count, code, lower):
    rows = leaf_map.shape[1]
    core = lax.axis_index("core")
    place = lax.broadcasted_iota(jnp.int32, (1, rows), 1)
    leaf = jnp.where(place < leaf_size[0], leaf_map[...], -1)
    parent = jnp.where(place < count[0], parent_map[...], -1)
    line = lax.broadcasted_iota(jnp.int32, (CODE_ROWS, rows), 0)
    digits = jnp.where(line < 2, leaf, parent)
    digits = jnp.where(line % 2 == 0, digits >> 5, digits & (DIGIT - 1))
    code[...] = (digits.astype(jnp.float32) + blank[...]).astype(jnp.bfloat16)
    lower[...] = picks((core,), leaf)


def product_kernel(fronts, omega, own_one, code, out, rest):
    rows = fronts.shape[1]
    mine = own_one.shape[1]
    out[rows : rows + mine, :] = own_one[0]
    out[rows + mine :, :] = code[...]
    partial = jnp.dot(fronts[0], omega[0], preferred_element_type=jnp.float32)
    high = partial.astype(jnp.bfloat16)
    out[:rows, :] = high
    rest[...] = (partial - high.astype(jnp.float32)).astype(jnp.bfloat16)


def decode(code):
    digits = code.astype(jnp.float32)
    leaf = digits[0:1] * DIGIT + digits[1:2]
    parent = digits[2:3] * DIGIT + digits[3:4]
    return leaf.astype(jnp.int32), parent.astype(jnp.int32)


def place_kernel(mine, rest, both, lower, out):
    rows = out.shape[2]
    block = out.shape[1] // 2
    n_row = rows // block
    core, row, here = lax.axis_index("core"), lax.axis_index("row"), lax.axis_index("y")
    other = both.at[1 - core]
    leaf, parent = decode(mine[rows + block :, :])
    other_leaf, other_parent = decode(other[rows + block :, :])
    other_lower = picks((core,), other_leaf)
    pages = [jnp.broadcast_to(half[:, k : k + LANES], (8, LANES)) for half in (parent, other_parent) for k in range(0, rows, LANES)]
    targets = []
    for index in (leaf, other_leaf):
        found = []
        for k in range(0, rows, LANES):
            at = jnp.broadcast_to(jnp.bitwise_xor(index[:, k : k + LANES], core * rows), (8, LANES))
            value = jnp.full((8, LANES), -1, jnp.int32)
            for page, entries in enumerate(pages):
                entry = jnp.take_along_axis(entries, at & (LANES - 1), axis=1, mode="promise_in_bounds")
                value = jnp.where(at >> 7 == page, entry, value)
            found.append(value[:1])
        targets.append(jnp.concatenate(found, axis=1))
    own = []
    for index in (parent, other_parent):
        turned = pltpu.roll(jnp.broadcast_to(index, (8, rows)), lax.rem(n_row - row, n_row) * block, 1)
        own.append(turned[:1, :block])
    own = jnp.concatenate(own, axis=1)
    line = lax.broadcasted_iota(jnp.int32, (rows, 2 * block), 0)
    partial = jnp.concatenate([mine[:rows, :], rest[...], other[:rows, :]], axis=0)
    pick = jnp.concatenate([lower[...], lower[...], other_lower], axis=1)
    level_one = jnp.dot(pick, partial, preferred_element_type=jnp.float32).astype(jnp.bfloat16)
    for x in range(n_row):
        out[2 * x + here, block:, :] = level_one[x * block : (x + 1) * block]
    partial = jnp.concatenate([partial, mine[rows : rows + block, :], other[rows : rows + block, :]], axis=0)
    for k, y in enumerate((here, 1 - here)):
        quarter = core + 2 * y
        picked = picks((quarter,), targets[0])
        pick = [picked, picked, picks((quarter,), targets[1]), (line + quarter * rows == own).astype(jnp.bfloat16)]
        placed = jnp.dot(jnp.concatenate(pick, axis=1), partial, preferred_element_type=jnp.float32)
        high = placed.astype(jnp.bfloat16)
        for x in range(n_row):
            out[2 * x + y, :block, :] = high[x * block : (x + 1) * block]
        if k == 1:
            low = (placed - high.astype(jnp.float32)).astype(jnp.bfloat16)
            for x in range(n_row):
                out[2 * x + y, block:, :] = low[x * block : (x + 1) * block]


def sum_kernel(pieces, message, own_two, one, two):
    n_row, rows = pieces.shape[0] // 2, pieces.shape[2]
    block = own_two.shape[1]
    y = lax.axis_index("y")
    total = message[rows : rows + block, :].astype(jnp.float32)
    for x in range(n_row):
        total += pieces[2 * x + y, block:, :].astype(jnp.float32)
    one[0] = total.astype(jnp.bfloat16)
    total = own_two[0].astype(jnp.float32)
    for k in range(2 * n_row):
        total += pieces[k, :block, :].astype(jnp.float32)
    for x in range(n_row):
        total += pieces[2 * x + 1 - y, block:, :].astype(jnp.float32)
    two[0] = total.astype(jnp.bfloat16)


def body(fronts, omega, leaf_sizes, leaf_map, own_one, parent_count, parent_map, own_two):
    _, rows, depth = fronts.shape
    cols = omega.shape[2]
    block = own_one.shape[1]
    n_row = rows // block
    params = pltpu.CompilerParams(vmem_limit_bytes=LIMIT)
    vmem, smem = whole(pltpu.VMEM), whole(pltpu.SMEM)
    near = lambda array: pltpu.with_memory_space_constraint(array, pltpu.VMEM)
    blank = pl.pallas_call(
        first_kernel,
        out_shape=pltpu.VMEM((CODE_ROWS, cols), jnp.float32),
        in_specs=[],
        out_specs=vmem,
        compiler_params=params,
        cost_estimate=pl.CostEstimate(flops=8 * 10**9, bytes_accessed=2**24, transcendentals=0),
        name="first",
    )()
    pick = pltpu.VMEM((rows, rows), jnp.bfloat16)
    code, lower = pl.pallas_call(
        index_kernel,
        out_shape=(pltpu.VMEM((CODE_ROWS, rows), jnp.bfloat16), pick),
        in_specs=[vmem] * 3 + [smem, smem],
        out_specs=(vmem,) * 2,
        compiler_params=params,
        name="index",
    )(near(blank), leaf_map, parent_map, leaf_sizes, parent_count)
    message, rest = pl.pallas_call(
        product_kernel,
        out_shape=(
            pltpu.VMEM((rows + block + CODE_ROWS, cols), jnp.bfloat16),
            pltpu.VMEM((rows, cols), jnp.bfloat16),
        ),
        in_specs=[vmem] * 4,
        out_specs=(vmem,) * 2,
        compiler_params=params,
        name="product",
    )(fronts, omega, own_one, near(code))
    both = lax.all_gather(message, "core")
    pieces = pl.pallas_call(
        place_kernel,
        out_shape=pltpu.VMEM((2 * n_row, 2 * block, cols), jnp.bfloat16),
        in_specs=[vmem] * 4,
        out_specs=vmem,
        compiler_params=params,
        name="place",
    )(near(message), near(rest), near(both), near(lower))
    pieces = lax.all_to_all(pieces, ("row", "y"), 0, 0)
    shape = jax.ShapeDtypeStruct(own_one.shape, jnp.bfloat16)
    return pl.pallas_call(
        sum_kernel,
        out_shape=(shape, shape),
        in_specs=[vmem, vmem, vmem],
        out_specs=(vmem, vmem),
        compiler_params=params,
        name="total",
    )(near(pieces), near(message), own_two)


def solution(mesh):
    n_cube, n_row = mesh.devices.shape
    grouped = Mesh(mesh.devices.reshape(n_cube // 4, 2, 2, n_row), ("group", "y", "core", "row"))
    cube = ("group", "y", "core")
    in_specs = (
        P(cube, None, "row"),
        P(cube, "row", None),
        P(cube),
        P(cube, None),
        P(cube, "row", None),
        P(cube),
        P(cube, None),
        P(cube, "row", None),
    )
    out_specs = (P(cube, "row", None), P(cube, "row", None))
    return jax.shard_map(body, mesh=grouped, in_specs=in_specs, out_specs=out_specs, check_vma=False)
```
